32 devices in a mesh: pipe: 4 (over z), tensor: 4 (over y, core), feat: 2 (over x).
Axes of the slice: x: 2, y: 2, z: 4, core: 2. Of those that a mesh axis runs over, the one named last changes fastest.
Arguments:
- cotangent: bfloat16 [256, 3584], P('feat', 'tensor'), may hold values from -6 to 6
- resid_in: bfloat16 [4, 256, 3584], P('pipe', 'feat', 'tensor'), may hold values from -6 to 6
- gate_pre: bfloat16 [4, 256, 7168], P('pipe', None, 'feat'), may hold values from -6 to 6
- up_pre: bfloat16 [4, 256, 7168], P('pipe', None, 'feat'), may hold values from -6 to 6
- w_gate: bfloat16 [4, 3584, 7168], P('pipe', 'tensor', 'feat'), may hold values from -0.09375 to 0.09375
- w_up: bfloat16 [4, 3584, 7168], P('pipe', 'tensor', 'feat'), may hold values from -0.09375 to 0.09375
- w_down: bfloat16 [4, 7168, 3584], P('pipe', 'feat', 'tensor'), may hold values from -0.0625 to 0.0625
- norm_gain: float32 [4, 3584], P('pipe', 'tensor'), may hold values from 0.25 to 1.75
- decoder: bfloat16 [4, 65536, 3584], P('pipe', 'feat', 'tensor'), may hold values from -0.09375 to 0.09375
- latent_ids: int32 [4, 256, 32], P('pipe'), may hold values from 0 to 65535
- latent_vals: float32 [4, 256, 32], P('pipe'), may hold values from 0.5 to 8
- attention_mask: int32 [256], replicated, may hold values from 0 to 1, as said below
Outputs:
- attribution: float32 [4, 65536], P('pipe', 'feat')
The draws below stay inside these ranges and needn't reach their ends.
Inputs may be any that keep to these rules, and one draw needn't show every extreme that they name: `attention_mask`: each of the 2 contexts of 128 tokens is live on a prefix; the first context is live throughout, every other one on 64 to 127 tokens.
All inputs are finite; a program needn't handle non-finite values.
Results may differ from the reference program's by a relative error of at most 0.015.
Values may be sent and summed in bfloat16 or wider, within the bound.
A program may use at most 320 MiB of HBM per device.

```python
import math
import jax
import jax.numpy as jnp
import numpy as np
from jax import lax

D = 3584
FF = 7168
LAT = 65536
ACTIVE = 32
CTX = 128
CTXS = 2
TOKENS = 256
LAYERS = 4


def draw_attention_mask(key, part):
    key = jax.random.fold_in(key, 11)
    live_len = jax.random.randint(key, (CTXS,), CTX // 2, CTX)
    live_len = live_len.at[0].set(CTX)
    position = jnp.arange(CTX, dtype=jnp.int32)
    return (position[None, :] < live_len[:, None]).astype(jnp.int32).reshape(TOKENS)


def with_ends(drawn, own_key, least, high):
    dims = drawn.shape
    index_at = [jax.random.randint(jax.random.fold_in(own_key, axis), (), 0, dims[axis]) for axis in range(len(dims))]
    drawn = drawn.at[tuple(index_at)].set(least)
    longest = dims.index(max(dims))
    index_at[longest] = (index_at[longest] + 1) % dims[longest]
    return drawn.at[tuple(index_at)].set(high)


def levels(key, shape, cuts, smallest, high):
    loudness, own = 1.0, jax.random.fold_in(key, 6)
    for dim, parts in cuts:
        steps = jnp.exp(jax.random.uniform(jax.random.fold_in(own, dim), (parts,), jnp.float32, smallest / len(cuts), high / len(cuts)))
        loudness = loudness * jnp.repeat(steps, shape[dim] // parts).reshape([-1 if axis == dim else 1 for axis in range(len(shape))])
    return loudness


def cumulative_ranks(count, lean):
    portions = [(1 << 20) // math.isqrt(grade ** lean) + 1 for grade in range(1, count + 1)]
    width = 1 + sum(portions) // (1 << 30)
    return np.cumsum(np.array([max(1, weight // width) for weight in portions]))


def ranked_ids(own_key, extent, number_of, slope):
    grid = cumulative_ranks(number_of, slope)
    ticket = jax.random.randint(jax.random.fold_in(own_key, 1), extent, 0, int(grid[number_of - 1]))
    rank = jnp.searchsorted(jnp.asarray(grid, jnp.int32), ticket, side="right")
    return jax.random.permutation(jax.random.fold_in(own_key, 2), number_of)[rank].astype(jnp.int32)


def normal_values(stream_key, shape, width, most, shards=(), kind=jnp.bfloat16):
    values = jax.random.normal(stream_key, shape, jnp.float32) * width
    if len(shards) > 0:
        values = levels(stream_key, shape, shards, -0.22, 0.18) * values
    return jnp.clip(values, min=-most, max=most).astype(kind)


def setup_inputs(seed: int = 0) -> dict:
    keys = jax.random.split(jax.random.key(seed), 13)
    cotangent = normal_values(keys[0], (TOKENS, D), 1.0, 6.0, ((0, 2), (1, 4)))
    resid_in = normal_values(keys[1], (LAYERS, TOKENS, D), 1.0, 6.0, ((0, 4), (1, 2), (2, 4)))
    gate_pre = normal_values(keys[2], (LAYERS, TOKENS, FF), 1.0, 6.0, ((0, 4), (2, 2)))
    up_pre = normal_values(keys[3], (LAYERS, TOKENS, FF), 1.0, 6.0, ((0, 4), (2, 2)))
    w_gate = normal_values(keys[4], (LAYERS, D, FF), D ** -0.5, 0.09375, ((0, 4), (1, 4), (2, 2)))
    w_up = normal_values(keys[5], (LAYERS, D, FF), D ** -0.5, 0.09375, ((0, 4), (1, 4), (2, 2)))
    w_down = normal_values(keys[6], (LAYERS, FF, D), FF ** -0.5, 0.0625, ((0, 4), (1, 2), (2, 4)))
    norm_gain = jnp.clip(1.0 + 0.15 * jax.random.normal(keys[7], (LAYERS, D), jnp.float32), 0.25, 1.75)
    decoder = normal_values(keys[8], (LAYERS, LAT, D), D ** -0.5, 0.09375, ((0, 4), (1, 2), (2, 4)))
    latent_ids = with_ends(ranked_ids(keys[9], (LAYERS, TOKENS, ACTIVE), LAT, 2), jax.random.fold_in(keys[9], 3), 0, LAT - 1).astype(jnp.int32)
    latent_vals = jnp.clip(jnp.exp(math.log(8.0) - 2.7725887 * jax.random.uniform(keys[10], (LAYERS, TOKENS, ACTIVE), jnp.float32) ** levels(keys[10], (LAYERS, TOKENS, ACTIVE), ((0, 4),), -0.2, 0.2)), 0.5, 8.0)
    attention_mask = draw_attention_mask(jax.random.fold_in(keys[12], 71), 0)
    return {"cotangent": cotangent, "resid_in": resid_in, "gate_pre": gate_pre, "up_pre": up_pre, "w_gate": w_gate, "w_up": w_up, "w_down": w_down, "norm_gain": norm_gain, "decoder": decoder, "latent_ids": latent_ids, "latent_vals": latent_vals, "attention_mask": attention_mask}


EPS = 1e-06

def gelu_pair(pre_act):
    return jax.vjp(lambda value: jax.nn.gelu(value, approximate=True), pre_act)

def layer_backward(grads, resid, gate, upper, w_gate, w_up, w_down, gain):
    hidden_grad = jnp.dot(grads, w_down.T, preferred_element_type=jnp.float32)
    active, pullback = gelu_pair(gate.astype(jnp.float32))
    gate_grad = pullback(hidden_grad * upper.astype(jnp.float32))[0].astype(jnp.bfloat16)
    up_grad = (hidden_grad * active).astype(jnp.bfloat16)
    normed_grad = jnp.dot(gate_grad, w_gate.T, preferred_element_type=jnp.float32) + jnp.dot(up_grad, w_up.T, preferred_element_type=jnp.float32)
    resid_f = resid.astype(jnp.float32)
    sq_sum = lax.optimization_barrier(jnp.sum(resid_f * resid_f, axis=1, keepdims=True))
    inner = lax.optimization_barrier(jnp.sum(normed_grad * gain * resid_f, axis=1, keepdims=True))
    scale = lax.rsqrt(sq_sum / D + EPS)
    result = grads.astype(jnp.float32) + gain * scale * normed_grad - resid_f * (scale * scale * scale) * inner / D
    return result.astype(jnp.bfloat16)

def reference(cotangent, resid_in, gate_pre, up_pre, w_gate, w_up, w_down, norm_gain, decoder, latent_ids, latent_vals, attention_mask):
    grads = cotangent
    live = attention_mask.astype(jnp.float32)
    results = []
    for layer in range(LAYERS - 1, -1, -1):
        grads = layer_backward(grads, resid_in[layer], gate_pre[layer], up_pre[layer], w_gate[layer], w_up[layer], w_down[layer], norm_gain[layer])
        chosen = jnp.take(decoder[layer], latent_ids[layer], axis=0)
        dots = jnp.einsum('tkd,td->tk', chosen.astype(jnp.float32), grads.astype(jnp.float32), precision=lax.Precision.HIGHEST)
        terms = latent_vals[layer] * live[:, None] * dots
        results.append(jax.ops.segment_sum(terms.reshape(-1), latent_ids[layer].reshape(-1), num_segments=LAT))
    results = results[::-1]
    return jnp.stack(results, axis=0)
```

```python
import functools

import jax
import jax.numpy as jnp
from jax import lax
from jax.experimental import pallas as pl
from jax.experimental.pallas import tpu as pltpu
from jax.sharding import PartitionSpec as P

EPS = 1e-06


def passed_along(value, axis, steps):
    count = lax.axis_size(axis)
    first, last = (max(0, -steps), min(count, count - steps))
    return lax.ppermute(value, axis, [(source, source + steps) for source in range(first, last)])


def gelu_pair(pre_act):
    return jax.vjp(lambda value: jax.nn.gelu(value, approximate=True), pre_act)


def layer_backward(grads, resid_own, gate, upper, w_gate, w_up, w_down, gain, feat_idx, row_share):
    width = grads.shape[1] * lax.axis_size("tensor")
    partial_hidden = lax.dot_general(
        grads, w_down, (((1,), (1,)), ((), ())), preferred_element_type=jnp.float32
    )
    hidden_grad = lax.psum(partial_hidden, "tensor")
    active, pullback = gelu_pair(gate.astype(jnp.float32))
    gate_grad = pullback(hidden_grad * upper.astype(jnp.float32))[0].astype(jnp.bfloat16)
    up_grad = (hidden_grad * active).astype(jnp.bfloat16)
    first = lax.dot_general(
        gate_grad, w_gate, (((1,), (1,)), ((), ())), preferred_element_type=jnp.float32
    )
    second = lax.dot_general(
        up_grad, w_up, (((1,), (1,)), ((), ())), preferred_element_type=jnp.float32
    )
    normed_grad = lax.psum_scatter(first + second, "feat", scatter_dimension=0, tiled=True)
    resid_f = resid_own.astype(jnp.float32)
    sq_part = jnp.sum(resid_f * resid_f, axis=1, keepdims=True)
    inner_part = jnp.sum(normed_grad * gain * resid_f, axis=1, keepdims=True)
    sq_sum, inner = lax.psum((sq_part, inner_part), "tensor")
    scale = lax.rsqrt(sq_sum / width + EPS)
    grads_own = lax.dynamic_slice_in_dim(grads, feat_idx * row_share, row_share, 0).astype(
        jnp.float32
    )
    result = (
        grads_own + gain * scale * normed_grad - resid_f * (scale * scale * scale) * inner / width
    )
    return lax.all_gather(result.astype(jnp.bfloat16), "feat", axis=0, tiled=True)


def on_device(
    cotangent,
    resid_in,
    gate_pre,
    up_pre,
    w_gate,
    w_up,
    w_down,
    norm_gain,
    decoder,
    latent_ids,
    latent_vals,
    attention_mask,
):
    feat_size = lax.axis_size("feat")
    pipe_size = lax.axis_size("pipe")
    section_idx = lax.axis_index("pipe")
    feat_idx = lax.axis_index("feat")
    cot_whole = lax.all_gather(cotangent, "feat", axis=0, tiled=True)
    tokens = gate_pre.shape[1]
    width_dev = cotangent.shape[1]
    pieces = 1
    row_share = tokens // (feat_size * pieces)

    def take_piece(whole_rows, step_piece):
        shaped = whole_rows.reshape(feat_size, pieces, row_share, whole_rows.shape[-1])
        picked = lax.dynamic_index_in_dim(shaped, step_piece, 1, keepdims=False)
        return picked.reshape(feat_size * row_share, whole_rows.shape[-1])

    resid_pieces = resid_in[0].reshape(pieces, row_share, width_dev)
    grad_store = jnp.zeros((feat_size, pieces, row_share, width_dev), jnp.bfloat16)
    received = jnp.zeros((feat_size * row_share, width_dev), jnp.bfloat16)
    is_top = section_idx == pipe_size - 1
    total_steps = pipe_size + pieces - 1
    for step in range(total_steps):
        piece_raw = step - (pipe_size - 1 - section_idx)
        is_valid = (piece_raw >= 0) & (piece_raw < pieces)
        step_piece = jnp.clip(piece_raw, 0, pieces - 1)
        incoming = jnp.where(is_top, take_piece(cot_whole, step_piece), received)
        resid_own = lax.dynamic_index_in_dim(resid_pieces, step_piece, 0, keepdims=False)
        outgoing = layer_backward(
            incoming,
            resid_own,
            take_piece(gate_pre[0], step_piece),
            take_piece(up_pre[0], step_piece),
            w_gate[0],
            w_up[0],
            w_down[0],
            norm_gain[0],
            feat_idx,
            row_share,
        )
        updated = lax.dynamic_update_index_in_dim(
            grad_store, outgoing.reshape(feat_size, 1, row_share, width_dev), step_piece, 1
        )
        grad_store = jnp.where(is_valid, updated, grad_store)
        if step + 1 < total_steps:
            received = passed_along(outgoing, "pipe", -1)
    layer_grads = grad_store.reshape(tokens, width_dev)
    lat_dev = decoder.shape[1]
    local_ix = latent_ids[0] - feat_idx * lat_dev
    inside = (local_ix >= 0) & (local_ix < lat_dev)
    live = attention_mask.astype(jnp.float32)
    act_weights = jnp.where(inside, latent_vals[0] * live[:, None], 0.0)
    slot_ix = jnp.clip(local_ix, 0, lat_dev - 1)
    token_ix = jnp.broadcast_to(jnp.arange(tokens, dtype=jnp.int32)[:, None], slot_ix.shape)
    dense_acts = jnp.zeros((tokens, lat_dev), jnp.float32).at[token_ix, slot_ix].add(act_weights)
    scores = lax.dot_general(
        layer_grads, decoder[0], (((1,), (1,)), ((), ())), preferred_element_type=jnp.float32
    )
    partial_value = jnp.sum(dense_acts * scores, axis=0)
    attribution = lax.psum(partial_value, "tensor")
    return attribution[None, :]


NT = (((1,), (1,)), ((), ()))
GROUP = 8
SQRT_2_OVER_PI = 0.7978845608028654
LO = 256
HIS_PER_STEP = 8


def chain_kernel(
    pieces, width, cot, resid, gate, upper, wg, wu, wd, gain, out,
    zin, resid_full, fac_gate, fac_up, s1, r1, acc, s2, r2, hid, nacc, sx, rx, msg_s, msg_r, res,
    zin_send, zin_recv, rs_send, rs_recv, y_send, y_recv, ag_send, ag_recv,
    x_send, x_recv, m_send, m_recv, z_send, resid_send, resid_recv,
):
    pipe, tensor, feat = lax.axis_index("pipe"), lax.axis_index("tensor"), lax.axis_index("feat")
    pipe_size = lax.axis_size("pipe")
    y, core = tensor // 2, lax.rem(tensor, 2)
    is_top, is_bottom = pipe == pipe_size - 1, pipe == 0
    tokens, ff = gate.shape
    rows = tokens // pieces
    own_rows = tokens // 2
    own_pieces = pieces // 2
    half = ff // 2
    core_peer = {"tensor": y * 2 + (1 - core)}
    y_peer = {"tensor": (1 - y) * 2 + core}
    x_peer = {"feat": 1 - feat}
    own_cols = pl.ds(pl.multiple_of(core * half, half), half)

    def group_peer(j):
        return {
            "tensor": lax.rem(y + (j // 2) % 2, 2) * 2 + lax.rem(core + j % 2, 2),
            "feat": lax.rem(feat + j // 4, 2),
        }

    def rows_of(p):
        return pl.ds(pl.multiple_of(p * rows, rows), rows)

    def send(src, dst, send_sem, recv_sem, device):
        return pltpu.make_async_remote_copy(
            src_ref=src, dst_ref=dst, send_sem=send_sem, recv_sem=recv_sem,
            device_id=device, device_id_type=pl.DeviceIdType.MESH,
        )

    def cot_copy(p):
        return send(zin.at[rows_of(p)], zin.at[rows_of(p)], zin_send.at[p], zin_recv.at[p], x_peer)

    own_part = pl.ds(pl.multiple_of(feat * own_rows, own_rows), own_rows)

    def resid_copy():
        return send(
            resid_full.at[own_part], resid_full.at[own_part],
            resid_send.at[0], resid_recv.at[0], x_peer,
        )

    def other_resid():
        part = pl.ds(pl.multiple_of((1 - feat) * own_rows, own_rows), own_rows)
        return send(
            resid_full.at[part], resid_full.at[part], resid_send.at[0], resid_recv.at[0], x_peer
        )

    def rs_copy(p):
        return send(s1.at[rows_of(p)], r1.at[rows_of(p)], rs_send.at[p], rs_recv.at[p], core_peer)

    def y_copy(p):
        return send(s2.at[rows_of(p)], r2.at[rows_of(p)], y_send.at[p], y_recv.at[p], y_peer)

    def ag_copy(p):
        part = hid.at[rows_of(p), own_cols]
        return send(part, part, ag_send.at[p], ag_recv.at[p], core_peer)

    def ag_arrival(p):
        part = hid.at[
            rows_of(p), pl.ds(pl.multiple_of((1 - core) * half, half), half)
        ]
        return send(part, part, ag_send.at[p], ag_recv.at[p], core_peer)

    def x_copy(p):
        return send(sx.at[rows_of(p)], rx.at[rows_of(p)], x_send.at[p], x_recv.at[p], x_peer)

    def m_copy(p, j):
        return send(
            msg_s.at[p], msg_r.at[p, j - 1], m_send.at[p, j - 1], m_recv.at[p, j - 1], group_peer(j)
        )

    def z_copy(p):
        return send(
            res.at[rows_of(p)], zin.at[rows_of(p)], z_send.at[p], zin_recv.at[p],
            {"pipe": jnp.maximum(pipe - 1, 0)},
        )

    barrier = pltpu.get_barrier_semaphore()
    for j in range(1, GROUP):
        pl.semaphore_signal(
            barrier, inc=1, device_id=group_peer(j), device_id_type=pl.DeviceIdType.MESH
        )

    @pl.when(jnp.logical_not(is_top))
    def _():
        pl.semaphore_signal(
            barrier, inc=1, device_id={"pipe": pipe + 1}, device_id_type=pl.DeviceIdType.MESH
        )

    @pl.when(jnp.logical_not(is_bottom))
    def _():
        pl.semaphore_signal(
            barrier, inc=1, device_id={"pipe": pipe - 1}, device_id_type=pl.DeviceIdType.MESH
        )

    neighbours = GROUP - 1 + jnp.minimum(pipe_size - 1 - pipe, 1) + jnp.minimum(pipe, 1)
    pl.semaphore_wait(barrier, neighbours)

    @pl.when(is_top)
    def _():
        zin[own_part, :] = cot[...]
        for i in range(own_pieces):
            cot_copy(feat * own_pieces + i).start()

    resid_full[own_part, :] = resid[...]
    resid_copy().start()

    def factors(p):
        part = 512

        @pl.loop(0, ff // part)
        def _(n):
            cols = pl.ds(pl.multiple_of(n * part, part), part)
            g = gate[rows_of(p), cols].astype(jnp.float32)
            u = upper[rows_of(p), cols].astype(jnp.float32)
            th = jnp.tanh(SQRT_2_OVER_PI * (g + 0.044715 * (g * g * g)))
            cdf = 0.5 * (1.0 + th)
            slope = cdf + (0.5 * SQRT_2_OVER_PI) * g * (1.0 - th * th) * (
                1.0 + (3.0 * 0.044715) * (g * g)
            )
            fac_gate[rows_of(p), cols] = slope * u
            fac_up[rows_of(p), cols] = g * cdf

    @pl.when(jnp.logical_not(is_top))
    def _():
        pl.loop(0, pieces)(factors)

    tile = 256

    def first_matmul(p):
        @pl.when(jnp.logical_not(is_top) | (p // own_pieces != feat))
        def _():
            z_copy(p).wait_recv()

        lhs = zin[rows_of(p), :]

        @pl.loop(0, half // tile)
        def _(n):
            at = pl.multiple_of((1 - core) * half + n * tile, tile)
            value = lax.dot_general(
                lhs, wd[pl.ds(at, tile), :], NT, preferred_element_type=jnp.float32
            )
            s1[rows_of(p), pl.ds(pl.multiple_of(n * tile, tile), tile)] = value.astype(jnp.bfloat16)

        rs_copy(p).start()

        @pl.loop(0, half // tile)
        def _(n):
            at = pl.multiple_of(core * half + n * tile, tile)
            acc[rows_of(p), pl.ds(pl.multiple_of(n * tile, tile), tile)] = lax.dot_general(
                lhs, wd[pl.ds(at, tile), :], NT, preferred_element_type=jnp.float32
            )

        @pl.when(is_top)
        def _():
            factors(p)

    def chip_sum(p):
        rs_copy(p).wait_recv()
        total = acc[rows_of(p), :] + r1[rows_of(p), :].astype(jnp.float32)
        acc[rows_of(p), :] = total
        s2[rows_of(p), :] = total.astype(jnp.bfloat16)
        y_copy(p).start()

    def pair_sum(p):
        y_copy(p).wait_recv()
        total = acc[rows_of(p), :] + r2[rows_of(p), :].astype(jnp.float32)
        hid[rows_of(p), own_cols] = total.astype(jnp.bfloat16)
        ag_copy(p).start()

    def second_matmul(p):
        ag_arrival(p).wait_recv()
        part = 512
        nacc[rows_of(p), :] = jnp.zeros((rows, nacc.shape[1]), jnp.float32)

        @pl.loop(0, ff // part)
        def _(n):
            cols = pl.ds(pl.multiple_of(n * part, part), part)
            h = hid[rows_of(p), cols].astype(jnp.float32)
            gg = (h * fac_gate[rows_of(p), cols]).astype(jnp.bfloat16)
            ug = (h * fac_up[rows_of(p), cols]).astype(jnp.bfloat16)
            nacc[rows_of(p), :] += lax.dot_general(
                gg, wg[:, cols], NT, preferred_element_type=jnp.float32
            ) + lax.dot_general(ug, wu[:, cols], NT, preferred_element_type=jnp.float32)

        part_sum = nacc[rows_of(p), :]
        sx[rows_of(p), :] = part_sum.astype(jnp.bfloat16)
        x_copy(p).start()
        res_f = resid_full[rows_of(p), :].astype(jnp.float32)
        inner = jnp.sum(part_sum * gain[...] * res_f, axis=1, keepdims=True)
        sq = 0.5 * jnp.sum(res_f * res_f, axis=1, keepdims=True)
        lane = lax.broadcasted_iota(jnp.int32, (rows, 128), 1)
        both = jnp.where(lane < 4, inner, sq)
        square = jnp.concatenate([both] * (128 // rows), axis=0)
        msg_s[p] = square.T[:8, :]
        for j in range(1, GROUP):
            m_copy(p, j).start()

    def finish(p):
        for j in range(1, GROUP):
            m_copy(p, j).wait_recv()
        total = msg_s[p]
        for j in range(1, GROUP):
            total = total + msg_r[p, j - 1]
        back = jnp.concatenate([total] * 16, axis=0).T
        inner, sq_sum = back[:rows, 0:1], back[:rows, 4:5]
        scale = lax.rsqrt(sq_sum / width + EPS)
        x_copy(p).wait_recv()
        normed = nacc[rows_of(p), :] + rx[rows_of(p), :].astype(jnp.float32)
        res_f = resid_full[rows_of(p), :].astype(jnp.float32)
        result = (
            zin[rows_of(p), :].astype(jnp.float32)
            + gain[...] * scale * normed
            - res_f * ((scale * scale * scale) * inner / width)
        ).astype(jnp.bfloat16)
        res[rows_of(p), :] = result

        @pl.when(jnp.logical_not(is_bottom))
        def _():
            z_copy(p).start()

        out[rows_of(p), :] = result

    @pl.loop(0, pieces + 2)
    def _(s):
        @pl.when(s < pieces)
        def _():
            first_matmul(s)

        @pl.when(s >= 2)
        def _():
            finish(s - 2)

        @pl.when((s >= 1) & (s <= pieces))
        def _():
            pair_sum(s - 1)

        @pl.when(s < pieces)
        def _():
            chip_sum(s)

        @pl.when(s == 1)
        def _():
            other_resid().wait_recv()

        @pl.when((s >= 1) & (s <= pieces))
        def _():
            second_matmul(s - 1)

    resid_copy().wait_send()

    @pl.when(is_top)
    def _():
        for i in range(own_pieces):
            cot_copy(feat * own_pieces + i).wait_send()

    @pl.loop(0, pieces)
    def _(p):
        rs_copy(p).wait_send()
        y_copy(p).wait_send()
        ag_copy(p).wait_send()
        x_copy(p).wait_send()
        for j in range(1, GROUP):
            m_copy(p, j).wait_send()

        @pl.when(jnp.logical_not(is_bottom))
        def _():
            z_copy(p).wait_send()


def chain(cotangent, resid, gate, upper, wg, wu, wd, gain):
    pieces = 4
    tokens, ff = gate.shape
    width_dev = cotangent.shape[1]
    half, rows = ff // 2, tokens // pieces
    width = width_dev * lax.axis_size("tensor")
    b16, f32 = jnp.bfloat16, jnp.float32
    dma = pltpu.SemaphoreType.DMA
    return pl.pallas_call(
        functools.partial(chain_kernel, pieces, width),
        out_shape=jax.ShapeDtypeStruct((tokens, width_dev), b16),
        in_specs=[pl.BlockSpec(memory_space=pltpu.VMEM)] * 8,
        out_specs=pl.BlockSpec(memory_space=pltpu.VMEM),
        scratch_shapes=[
            pltpu.VMEM((tokens, width_dev), b16),
            pltpu.VMEM((tokens, width_dev), b16),
            pltpu.VMEM((tokens, ff), f32),
            pltpu.VMEM((tokens, ff), f32),
            pltpu.VMEM((tokens, half), b16),
            pltpu.VMEM((tokens, half), b16),
            pltpu.VMEM((tokens, half), f32),
            pltpu.VMEM((tokens, half), b16),
            pltpu.VMEM((tokens, half), b16),
            pltpu.VMEM((tokens, ff), b16),
            pltpu.VMEM((tokens, width_dev), f32),
            pltpu.VMEM((tokens, width_dev), b16),
            pltpu.VMEM((tokens, width_dev), b16),
            pltpu.VMEM((pieces, 8, 128), f32),
            pltpu.VMEM((pieces, GROUP - 1, 8, 128), f32),
            pltpu.VMEM((tokens, width_dev), b16),
        ]
        + [dma((pieces,))] * 10
        + [dma((pieces, GROUP - 1))] * 2
        + [dma((pieces,)), dma((1,)), dma((1,))],
        compiler_params=pltpu.CompilerParams(
            collective_id=0, has_side_effects=True, vmem_limit_bytes=58 * 2**20
        ),
        name="chain",
    )(cotangent, resid, gate, upper, wg, wu, wd, gain)


def score_kernel(grads, hi_ids, lo_ids, weights, dec, out, *dense):
    tokens = grads.shape[0]
    his = dense[0].shape[0] // tokens
    slots = hi_ids.shape[1]

    @pl.when(pl.program_id(0) == 0)
    def _():
        @pl.loop(0, tokens, unroll=4)
        def _(t):
            at = pl.ds(t, 1)
            hi = lax.broadcasted_iota(jnp.int32, (his, slots), 0) == hi_ids[at, :]
            lo = lax.broadcasted_iota(jnp.int32, (LO, slots), 0) == lo_ids[at, :]
            lhs = jnp.where(hi, weights[at, :], 0.0).astype(jnp.bfloat16)
            rhs = jnp.where(lo, 1.0, 0.0).astype(jnp.bfloat16)
            value = lax.dot_general(lhs, rhs, NT, preferred_element_type=jnp.float32)
            for n, ref in enumerate(dense):
                ref[pl.ds(t, his, stride=tokens), :] = value[:, n * 128 : (n + 1) * 128]

    first = pl.program_id(0) * HIS_PER_STEP
    for j in range(HIS_PER_STEP):
        scores = lax.dot_general(
            grads[...], dec[j * LO : (j + 1) * LO, :], NT, preferred_element_type=jnp.float32
        )
        at = pl.ds(pl.multiple_of((first + j) * tokens, tokens), tokens)
        for n, ref in enumerate(dense):
            cols = slice(n * 128, (n + 1) * 128)
            out[j : j + 1, cols] = jnp.sum(ref[at, :] * scores[:, cols], axis=0, keepdims=True)


def score(grads, decoder, ids, weights):
    tokens, width_dev = grads.shape
    his = decoder.shape[0] // LO
    coarse = weights.astype(jnp.bfloat16).astype(jnp.float32)
    parts = jnp.concatenate([coarse, weights - coarse], axis=1)
    both = jnp.concatenate([ids, ids], axis=1)
    slots = both.shape[1]
    fixed = lambda shape: pl.BlockSpec(shape, lambda i: (0, 0))
    return pl.pallas_call(
        score_kernel,
        grid=(his // HIS_PER_STEP,),
        out_shape=jax.ShapeDtypeStruct((his, LO), jnp.float32),
        in_specs=[
            fixed((tokens, width_dev)),
            fixed((tokens, slots)),
            fixed((tokens, slots)),
            fixed((tokens, slots)),
            pl.BlockSpec((HIS_PER_STEP * LO, width_dev), lambda i: (i, 0)),
        ],
        out_specs=pl.BlockSpec((HIS_PER_STEP, LO), lambda i: (i, 0)),
        scratch_shapes=[pltpu.VMEM((his * tokens, 128), jnp.float32)] * (LO // 128),
        compiler_params=pltpu.CompilerParams(vmem_limit_bytes=58 * 2**20),
        name="score",
    )(grads, both // LO, both % LO, parts, decoder)


def width_sum_kernel(part, out, mid, r1, r2, send_sem, recv_sem):
    tensor = lax.axis_index("tensor")
    y, core = tensor // 2, lax.rem(tensor, 2)
    peers = ({"tensor": y * 2 + (1 - core)}, {"tensor": (1 - y) * 2 + core})
    barrier = pltpu.get_barrier_semaphore()
    for peer in peers:
        pl.semaphore_signal(barrier, inc=1, device_id=peer, device_id_type=pl.DeviceIdType.MESH)
    pl.semaphore_wait(barrier, 2)

    def copy(src, dst, i):
        return pltpu.make_async_remote_copy(
            src_ref=src, dst_ref=dst, send_sem=send_sem.at[i], recv_sem=recv_sem.at[i],
            device_id=peers[i], device_id_type=pl.DeviceIdType.MESH,
        )

    first = copy(part, r1, 0)
    first.start()
    first.wait()
    mid[...] = part[...] + r1[...]
    second = copy(mid, r2, 1)
    second.start()
    second.wait()
    out[...] = mid[...] + r2[...]


def width_sum(part):
    buffer = pltpu.VMEM(part.shape, part.dtype)
    return pl.pallas_call(
        width_sum_kernel,
        out_shape=jax.ShapeDtypeStruct(part.shape, part.dtype),
        in_specs=[pl.BlockSpec(memory_space=pltpu.VMEM)],
        out_specs=pl.BlockSpec(memory_space=pltpu.VMEM),
        scratch_shapes=[buffer] * 3 + [pltpu.SemaphoreType.DMA((2,))] * 2,
        compiler_params=pltpu.CompilerParams(collective_id=1, has_side_effects=True),
        name="width_sum",
    )(part)


def on_device_pairs(
    cotangent,
    resid_in,
    gate_pre,
    up_pre,
    w_gate,
    w_up,
    w_down,
    norm_gain,
    decoder,
    latent_ids,
    latent_vals,
    attention_mask,
):
    grads = chain(
        cotangent, resid_in[0], gate_pre[0], up_pre[0], w_gate[0], w_up[0], w_down[0], norm_gain
    )
    lat_dev = decoder.shape[1]
    local_ix = latent_ids[0] - lax.axis_index("feat") * lat_dev
    inside = (local_ix >= 0) & (local_ix < lat_dev)
    live = attention_mask.astype(jnp.float32)
    weights = jnp.where(inside, latent_vals[0] * live[:, None], 0.0)
    slot_ix = jnp.clip(local_ix, 0, lat_dev - 1)
    return width_sum(score(grads, decoder[0], slot_ix, weights)).reshape(1, lat_dev)


def solution(mesh):
    in_pairs = mesh.shape["tensor"] == 4 and mesh.shape["feat"] == 2
    body = on_device_pairs if in_pairs else on_device
    return jax.shard_map(
        body,
        mesh=mesh,
        in_specs=(
            P("feat", "tensor"),
            P("pipe", "feat", "tensor"),
            P("pipe", None, "feat"),
            P("pipe", None, "feat"),
            P("pipe", "tensor", "feat"),
            P("pipe", "tensor", "feat"),
            P("pipe", "feat", "tensor"),
            P("pipe", "tensor"),
            P("pipe", "feat", "tensor"),
            P("pipe", None, None),
            P("pipe", None, None),
            P(),
        ),
        out_specs=P("pipe", "feat"),
        check_vma=False,
    )
```

```python
import functools

import jax
import jax.numpy as jnp
from jax import lax
from jax.experimental import pallas as pl
from jax.experimental.pallas import tpu as pltpu
from jax.sharding import PartitionSpec as P

EPS = 1e-06


def passed_along(value, axis, steps):
    count = lax.axis_size(axis)
    first, last = (max(0, -steps), min(count, count - steps))
    return lax.ppermute(value, axis, [(source, source + steps) for source in range(first, last)])


def gelu_pair(pre_act):
    return jax.vjp(lambda value: jax.nn.gelu(value, approximate=True), pre_act)


def layer_backward(grads, resid_own, gate, upper, w_gate, w_up, w_down, gain, feat_idx, row_share):
    width = grads.shape[1] * lax.axis_size("tensor")
    partial_hidden = lax.dot_general(
        grads, w_down, (((1,), (1,)), ((), ())), preferred_element_type=jnp.float32
    )
    hidden_grad = lax.psum(partial_hidden, "tensor")
    active, pullback = gelu_pair(gate.astype(jnp.float32))
    gate_grad = pullback(hidden_grad * upper.astype(jnp.float32))[0].astype(jnp.bfloat16)
    up_grad = (hidden_grad * active).astype(jnp.bfloat16)
    first = lax.dot_general(
        gate_grad, w_gate, (((1,), (1,)), ((), ())), preferred_element_type=jnp.float32
    )
    second = lax.dot_general(
        up_grad, w_up, (((1,), (1,)), ((), ())), preferred_element_type=jnp.float32
    )
    normed_grad = lax.psum_scatter(first + second, "feat", scatter_dimension=0, tiled=True)
    resid_f = resid_own.astype(jnp.float32)
    sq_part = jnp.sum(resid_f * resid_f, axis=1, keepdims=True)
    inner_part = jnp.sum(normed_grad * gain * resid_f, axis=1, keepdims=True)
    sq_sum, inner = lax.psum((sq_part, inner_part), "tensor")
    scale = lax.rsqrt(sq_sum / width + EPS)
    grads_own = lax.dynamic_slice_in_dim(grads, feat_idx * row_share, row_share, 0).astype(
        jnp.float32
    )
    result = (
        grads_own + gain * scale * normed_grad - resid_f * (scale * scale * scale) * inner / width
    )
    return lax.all_gather(result.astype(jnp.bfloat16), "feat", axis=0, tiled=True)


def on_device(
    cotangent,
    resid_in,
    gate_pre,
    up_pre,
    w_gate,
    w_up,
    w_down,
    norm_gain,
    decoder,
    latent_ids,
    latent_vals,
    attention_mask,
):
    feat_size = lax.axis_size("feat")
    pipe_size = lax.axis_size("pipe")
    section_idx = lax.axis_index("pipe")
    feat_idx = lax.axis_index("feat")
    cot_whole = lax.all_gather(cotangent, "feat", axis=0, tiled=True)
    tokens = gate_pre.shape[1]
    width_dev = cotangent.shape[1]
    pieces = 1
    row_share = tokens // (feat_size * pieces)

    def take_piece(whole_rows, step_piece):
        shaped = whole_rows.reshape(feat_size, pieces, row_share, whole_rows.shape[-1])
        picked = lax.dynamic_index_in_dim(shaped, step_piece, 1, keepdims=False)
        return picked.reshape(feat_size * row_share, whole_rows.shape[-1])

    resid_pieces = resid_in[0].reshape(pieces, row_share, width_dev)
    grad_store = jnp.zeros((feat_size, pieces, row_share, width_dev), jnp.bfloat16)
    received = jnp.zeros((feat_size * row_share, width_dev), jnp.bfloat16)
    is_top = section_idx == pipe_size - 1
    total_steps = pipe_size + pieces - 1
    for step in range(total_steps):
        piece_raw = step - (pipe_size - 1 - section_idx)
        is_valid = (piece_raw >= 0) & (piece_raw < pieces)
        step_piece = jnp.clip(piece_raw, 0, pieces - 1)
        incoming = jnp.where(is_top, take_piece(cot_whole, step_piece), received)
        resid_own = lax.dynamic_index_in_dim(resid_pieces, step_piece, 0, keepdims=False)
        outgoing = layer_backward(
            incoming,
            resid_own,
            take_piece(gate_pre[0], step_piece),
            take_piece(up_pre[0], step_piece),
            w_gate[0],
            w_up[0],
            w_down[0],
            norm_gain[0],
            feat_idx,
            row_share,
        )
        updated = lax.dynamic_update_index_in_dim(
            grad_store, outgoing.reshape(feat_size, 1, row_share, width_dev), step_piece, 1
        )
        grad_store = jnp.where(is_valid, updated, grad_store)
        if step + 1 < total_steps:
            received = passed_along(outgoing, "pipe", -1)
    layer_grads = grad_store.reshape(tokens, width_dev)
    lat_dev = decoder.shape[1]
    local_ix = latent_ids[0] - feat_idx * lat_dev
    inside = (local_ix >= 0) & (local_ix < lat_dev)
    live = attention_mask.astype(jnp.float32)
    act_weights = jnp.where(inside, latent_vals[0] * live[:, None], 0.0)
    slot_ix = jnp.clip(local_ix, 0, lat_dev - 1)
    token_ix = jnp.broadcast_to(jnp.arange(tokens, dtype=jnp.int32)[:, None], slot_ix.shape)
    dense_acts = jnp.zeros((tokens, lat_dev), jnp.float32).at[token_ix, slot_ix].add(act_weights)
    scores = lax.dot_general(
        layer_grads, decoder[0], (((1,), (1,)), ((), ())), preferred_element_type=jnp.float32
    )
    partial_value = jnp.sum(dense_acts * scores, axis=0)
    attribution = lax.psum(partial_value, "tensor")
    return attribution[None, :]


NT = (((1,), (1,)), ((), ()))
GROUP = 8
SQRT_2_OVER_PI = 0.7978845608028654
LO = 256
HIS_PER_STEP = 8


def chain_kernel(
    pieces, width, cot, resid, gate, upper, wg, wu, wd, gain, out,
    zin, resid_full, fac_gate, fac_up, s1, r1, acc, s2, r2, hid, nacc, sx, rx, msg_s, msg_r, res,
    zin_send, zin_recv, rs_send, rs_recv, y_send, y_recv, ag_send, ag_recv,
    x_send, x_recv, m_send, m_recv, z_send, resid_send, resid_recv,
):
    pipe, tensor, feat = lax.axis_index("pipe"), lax.axis_index("tensor"), lax.axis_index("feat")
    pipe_size = lax.axis_size("pipe")
    y, core = tensor // 2, lax.rem(tensor, 2)
    is_top, is_bottom = pipe == pipe_size - 1, pipe == 0
    tokens, ff = gate.shape
    rows = tokens // pieces
    own_rows = tokens // 2
    own_pieces = pieces // 2
    half = ff // 2
    core_peer = {"tensor": y * 2 + (1 - core)}
    y_peer = {"tensor": (1 - y) * 2 + core}
    x_peer = {"feat": 1 - feat}
    own_cols = pl.ds(pl.multiple_of(core * half, half), half)

    def group_peer(j):
        return {
            "tensor": lax.rem(y + (j // 2) % 2, 2) * 2 + lax.rem(core + j % 2, 2),
            "feat": lax.rem(feat + j // 4, 2),
        }

    def rows_of(p):
        return pl.ds(pl.multiple_of(p * rows, rows), rows)

    def send(src, dst, send_sem, recv_sem, device):
        return pltpu.make_async_remote_copy(
            src_ref=src, dst_ref=dst, send_sem=send_sem, recv_sem=recv_sem,
            device_id=device, device_id_type=pl.DeviceIdType.MESH,
        )

    def cot_copy(p):
        return send(zin.at[rows_of(p)], zin.at[rows_of(p)], zin_send.at[p], zin_recv.at[p], x_peer)

    own_part = pl.ds(pl.multiple_of(feat * own_rows, own_rows), own_rows)

    def resid_copy():
        return send(
            resid_full.at[own_part], resid_full.at[own_part],
            resid_send.at[0], resid_recv.at[0], x_peer,
        )

    def other_resid():
        part = pl.ds(pl.multiple_of((1 - feat) * own_rows, own_rows), own_rows)
        return send(
            resid_full.at[part], resid_full.at[part], resid_send.at[0], resid_recv.at[0], x_peer
        )

    def rs_copy(p):
        return send(s1.at[rows_of(p)], r1.at[rows_of(p)], rs_send.at[p], rs_recv.at[p], core_peer)

    def y_copy(p):
        return send(s2.at[rows_of(p)], r2.at[rows_of(p)], y_send.at[p], y_recv.at[p], y_peer)

    def ag_copy(p):
        part = hid.at[rows_of(p), own_cols]
        return send(part, part, ag_send.at[p], ag_recv.at[p], core_peer)

    def ag_arrival(p):
        part = hid.at[
            rows_of(p), pl.ds(pl.multiple_of((1 - core) * half, half), half)
        ]
        return send(part, part, ag_send.at[p], ag_recv.at[p], core_peer)

    def x_copy(p):
        return send(sx.at[rows_of(p)], rx.at[rows_of(p)], x_send.at[p], x_recv.at[p], x_peer)

    def m_copy(p, j):
        return send(
            msg_s.at[p], msg_r.at[p, j - 1], m_send.at[p, j - 1], m_recv.at[p, j - 1], group_peer(j)
        )

    def z_copy(p):
        return send(
            res.at[rows_of(p)], zin.at[rows_of(p)], z_send.at[p], zin_recv.at[p],
            {"pipe": jnp.maximum(pipe - 1, 0)},
        )

    barrier = pltpu.get_barrier_semaphore()
    for j in range(1, GROUP):
        pl.semaphore_signal(
            barrier, inc=1, device_id=group_peer(j), device_id_type=pl.DeviceIdType.MESH
        )

    @pl.when(jnp.logical_not(is_top))
    def _():
        pl.semaphore_signal(
            barrier, inc=1, device_id={"pipe": pipe + 1}, device_id_type=pl.DeviceIdType.MESH
        )

    @pl.when(jnp.logical_not(is_bottom))
    def _():
        pl.semaphore_signal(
            barrier, inc=1, device_id={"pipe": pipe - 1}, device_id_type=pl.DeviceIdType.MESH
        )

    neighbours = GROUP - 1 + jnp.minimum(pipe_size - 1 - pipe, 1) + jnp.minimum(pipe, 1)
    pl.semaphore_wait(barrier, neighbours)

    @pl.when(is_top)
    def _():
        zin[own_part, :] = cot[...]
        for i in range(own_pieces):
            cot_copy(feat * own_pieces + i).start()

    resid_full[own_part, :] = resid[...]
    resid_copy().start()

    def factors(p):
        part = 512

        @pl.loop(0, ff // part)
        def _(n):
            cols = pl.ds(pl.multiple_of(n * part, part), part)
            g = gate[rows_of(p), cols].astype(jnp.float32)
            u = upper[rows_of(p), cols].astype(jnp.float32)
            th = jnp.tanh(SQRT_2_OVER_PI * (g + 0.044715 * (g * g * g)))
            cdf = 0.5 * (1.0 + th)
            slope = cdf + (0.5 * SQRT_2_OVER_PI) * g * (1.0 - th * th) * (
                1.0 + (3.0 * 0.044715) * (g * g)
            )
            fac_gate[rows_of(p), cols] = slope * u
            fac_up[rows_of(p), cols] = g * cdf

    @pl.when(jnp.logical_not(is_top))
    def _():
        pl.loop(0, pieces)(factors)

    tile = half // 2

    def first_matmul(p):
        @pl.when(jnp.logical_not(is_top) | (p // own_pieces != feat))
        def _():
            z_copy(p).wait_recv()

        lhs = zin[rows_of(p), :]

        @pl.loop(0, half // tile)
        def _(n):
            at = pl.multiple_of((1 - core) * half + n * tile, tile)
            value = lax.dot_general(
                lhs, wd[pl.ds(at, tile), :], NT, preferred_element_type=jnp.float32
            )
            s1[rows_of(p), pl.ds(pl.multiple_of(n * tile, tile), tile)] = value.astype(jnp.bfloat16)

        rs_copy(p).start()

        @pl.loop(0, half // tile)
        def _(n):
            at = pl.multiple_of(core * half + n * tile, tile)
            acc[rows_of(p), pl.ds(pl.multiple_of(n * tile, tile), tile)] = lax.dot_general(
                lhs, wd[pl.ds(at, tile), :], NT, preferred_element_type=jnp.float32
            )

        @pl.when(is_top)
        def _():
            factors(p)

    def chip_sum(p):
        rs_copy(p).wait_recv()
        total = acc[rows_of(p), :] + r1[rows_of(p), :].astype(jnp.float32)
        acc[rows_of(p), :] = total
        s2[rows_of(p), :] = total.astype(jnp.bfloat16)
        y_copy(p).start()

    def pair_sum(p):
        y_copy(p).wait_recv()
        total = acc[rows_of(p), :] + r2[rows_of(p), :].astype(jnp.float32)
        hid[rows_of(p), own_cols] = total.astype(jnp.bfloat16)
        ag_copy(p).start()

    def second_matmul(p):
        ag_arrival(p).wait_recv()
        part = half
        nacc[rows_of(p), :] = jnp.zeros((rows, nacc.shape[1]), jnp.float32)

        @pl.loop(0, ff // part)
        def _(n):
            cols = pl.ds(pl.multiple_of(n * part, part), part)
            h = hid[rows_of(p), cols].astype(jnp.float32)
            gg = (h * fac_gate[rows_of(p), cols]).astype(jnp.bfloat16)
            ug = (h * fac_up[rows_of(p), cols]).astype(jnp.bfloat16)
            nacc[rows_of(p), :] += lax.dot_general(
                gg, wg[:, cols], NT, preferred_element_type=jnp.float32
            ) + lax.dot_general(ug, wu[:, cols], NT, preferred_element_type=jnp.float32)

        part_sum = nacc[rows_of(p), :]
        sx[rows_of(p), :] = part_sum.astype(jnp.bfloat16)
        x_copy(p).start()
        res_f = resid_full[rows_of(p), :].astype(jnp.float32)
        inner = jnp.sum(part_sum * gain[...] * res_f, axis=1, keepdims=True)
        sq = 0.5 * jnp.sum(res_f * res_f, axis=1, keepdims=True)
        lane = lax.broadcasted_iota(jnp.int32, (rows, 128), 1)
        both = jnp.where(lane < 4, inner, sq)
        square = jnp.concatenate([both] * (128 // rows), axis=0)
        msg_s[p] = square.T[:8, :]
        for j in range(1, GROUP):
            m_copy(p, j).start()

    def finish(p):
        for j in range(1, GROUP):
            m_copy(p, j).wait_recv()
        total = msg_s[p]
        for j in range(1, GROUP):
            total = total + msg_r[p, j - 1]
        back = jnp.concatenate([total] * 16, axis=0).T
        inner, sq_sum = back[:rows, 0:1], back[:rows, 4:5]
        scale = lax.rsqrt(sq_sum / width + EPS)
        x_copy(p).wait_recv()
        normed = nacc[rows_of(p), :] + rx[rows_of(p), :].astype(jnp.float32)
        res_f = resid_full[rows_of(p), :].astype(jnp.float32)
        result = (
            zin[rows_of(p), :].astype(jnp.float32)
            + gain[...] * scale * normed
            - res_f * ((scale * scale * scale) * inner / width)
        ).astype(jnp.bfloat16)
        res[rows_of(p), :] = result

        @pl.when(jnp.logical_not(is_bottom))
        def _():
            z_copy(p).start()

        out[rows_of(p), :] = result

    @pl.loop(0, pieces + 2)
    def _(s):
        @pl.when(s < pieces)
        def _():
            first_matmul(s)

        @pl.when(s >= 2)
        def _():
            finish(s - 2)

        @pl.when((s >= 1) & (s <= pieces))
        def _():
            pair_sum(s - 1)

        @pl.when(s < pieces)
        def _():
            chip_sum(s)

        @pl.when(s == 1)
        def _():
            other_resid().wait_recv()

        @pl.when((s >= 1) & (s <= pieces))
        def _():
            second_matmul(s - 1)

    resid_copy().wait_send()

    @pl.when(is_top)
    def _():
        for i in range(own_pieces):
            cot_copy(feat * own_pieces + i).wait_send()

    @pl.loop(0, pieces)
    def _(p):
        rs_copy(p).wait_send()
        y_copy(p).wait_send()
        ag_copy(p).wait_send()
        x_copy(p).wait_send()
        for j in range(1, GROUP):
            m_copy(p, j).wait_send()

        @pl.when(jnp.logical_not(is_bottom))
        def _():
            z_copy(p).wait_send()


def chain(cotangent, resid, gate, upper, wg, wu, wd, gain):
    pieces = 4
    tokens, ff = gate.shape
    width_dev = cotangent.shape[1]
    half, rows = ff // 2, tokens // pieces
    width = width_dev * lax.axis_size("tensor")
    b16, f32 = jnp.bfloat16, jnp.float32
    dma = pltpu.SemaphoreType.DMA
    return pl.pallas_call(
        functools.partial(chain_kernel, pieces, width),
        out_shape=jax.ShapeDtypeStruct((tokens, width_dev), b16),
        in_specs=[pl.BlockSpec(memory_space=pltpu.VMEM)] * 8,
        out_specs=pl.BlockSpec(memory_space=pltpu.VMEM),
        scratch_shapes=[
            pltpu.VMEM((tokens, width_dev), b16),
            pltpu.VMEM((tokens, width_dev), b16),
            pltpu.VMEM((tokens, ff), f32),
            pltpu.VMEM((tokens, ff), f32),
            pltpu.VMEM((tokens, half), b16),
            pltpu.VMEM((tokens, half), b16),
            pltpu.VMEM((tokens, half), f32),
            pltpu.VMEM((tokens, half), b16),
            pltpu.VMEM((tokens, half), b16),
            pltpu.VMEM((tokens, ff), b16),
            pltpu.VMEM((tokens, width_dev), f32),
            pltpu.VMEM((tokens, width_dev), b16),
            pltpu.VMEM((tokens, width_dev), b16),
            pltpu.VMEM((pieces, 8, 128), f32),
            pltpu.VMEM((pieces, GROUP - 1, 8, 128), f32),
            pltpu.VMEM((tokens, width_dev), b16),
        ]
        + [dma((pieces,))] * 10
        + [dma((pieces, GROUP - 1))] * 2
        + [dma((pieces,)), dma((1,)), dma((1,))],
        compiler_params=pltpu.CompilerParams(
            collective_id=0, has_side_effects=True, vmem_limit_bytes=58 * 2**20
        ),
        name="chain",
    )(cotangent, resid, gate, upper, wg, wu, wd, gain)


def acts_kernel(early, hi_ids, lo_ids, weights, *refs):
    out, left, right, stage, sem = refs[-5:]
    tokens, slots = hi_ids.shape
    his = left.shape[0] // tokens
    is_early = lax.axis_index("pipe") < lax.axis_size("pipe") - 2

    @pl.when(is_early if early else jnp.logical_not(is_early))
    def _():
        @pl.loop(0, tokens, unroll=4)
        def _(t):
            at = pl.ds(t, 1)
            hi = lax.broadcasted_iota(jnp.int32, (his, slots), 0) == hi_ids[at, :]
            lo = lax.broadcasted_iota(jnp.int32, (LO, slots), 0) == lo_ids[at, :]
            lhs = jnp.where(hi, weights[at, :], 0.0).astype(jnp.bfloat16)
            rhs = jnp.where(lo, 1.0, 0.0).astype(jnp.bfloat16)
            value = lax.dot_general(lhs, rhs, NT, preferred_element_type=jnp.float32)
            left[pl.ds(t, his, stride=tokens), :] = value[:, :128]
            right[pl.ds(t, his, stride=tokens), :] = value[:, 128:]

        block = stage.shape[1]

        def copy(n):
            slot = lax.rem(n, 2)
            at = pl.ds(pl.multiple_of(n * block, block), block)
            return pltpu.make_async_copy(stage.at[slot], out.at[at], sem.at[slot])

        steps = his * tokens // block

        @pl.loop(0, steps)
        def _(n):
            @pl.when(n >= 2)
            def _():
                copy(n - 2).wait()

            at = pl.ds(pl.multiple_of(n * block, block), block)
            stage[lax.rem(n, 2), :, 0:128] = left[at, :].astype(jnp.bfloat16)
            stage[lax.rem(n, 2), :, 128:256] = right[at, :].astype(jnp.bfloat16)
            copy(n).start()

        copy(steps - 2).wait()
        copy(steps - 1).wait()


def build_acts(his, both, parts, *before):
    early = not before
    tokens = both.shape[0]
    block = HIS_PER_STEP * tokens
    in_vmem = pl.BlockSpec(memory_space=pltpu.VMEM)
    anywhere = pl.BlockSpec(memory_space=pl.ANY)
    return pl.pallas_call(
        functools.partial(acts_kernel, early),
        out_shape=jax.ShapeDtypeStruct((his * tokens, LO), jnp.bfloat16),
        in_specs=[in_vmem] * 3 + [anywhere] * len(before),
        out_specs=anywhere,
        input_output_aliases={3: 0} if before else {},
        scratch_shapes=[pltpu.VMEM((his * tokens, 128), jnp.float32)] * 2
        + [pltpu.VMEM((2, block, LO), jnp.bfloat16), pltpu.SemaphoreType.DMA((2,))],
        compiler_params=pltpu.CompilerParams(vmem_limit_bytes=58 * 2**20),
        name="acts_early" if early else "acts_late",
    )(both // LO, both % LO, parts, *before)


def score_kernel(grads, acts, dec, out):
    tokens = grads.shape[0]
    for j in range(HIS_PER_STEP):
        scores = lax.dot_general(
            grads[...], dec[j * LO : (j + 1) * LO, :], NT, preferred_element_type=jnp.float32
        )
        own = acts[j * tokens : (j + 1) * tokens, :].astype(jnp.float32)
        out[j : j + 1, :] = jnp.sum(own * scores, axis=0, keepdims=True)


def score(grads, decoder, acts):
    tokens, width_dev = grads.shape
    his = decoder.shape[0] // LO
    return pl.pallas_call(
        score_kernel,
        grid=(his // HIS_PER_STEP,),
        out_shape=jax.ShapeDtypeStruct((his, LO), jnp.float32),
        in_specs=[
            pl.BlockSpec((tokens, width_dev), lambda i: (0, 0)),
            pl.BlockSpec((HIS_PER_STEP * tokens, LO), lambda i: (i, 0)),
            pl.BlockSpec((HIS_PER_STEP * LO, width_dev), lambda i: (i, 0)),
        ],
        out_specs=pl.BlockSpec((HIS_PER_STEP, LO), lambda i: (i, 0)),
        compiler_params=pltpu.CompilerParams(vmem_limit_bytes=40 * 2**20),
        name="score",
    )(grads, acts, decoder)


def width_sum_kernel(part, out, mid, r1, r2, send_sem, recv_sem):
    tensor = lax.axis_index("tensor")
    y, core = tensor // 2, lax.rem(tensor, 2)
    peers = ({"tensor": y * 2 + (1 - core)}, {"tensor": (1 - y) * 2 + core})
    barrier = pltpu.get_barrier_semaphore()
    for peer in peers:
        pl.semaphore_signal(barrier, inc=1, device_id=peer, device_id_type=pl.DeviceIdType.MESH)
    pl.semaphore_wait(barrier, 2)

    def copy(src, dst, i):
        return pltpu.make_async_remote_copy(
            src_ref=src, dst_ref=dst, send_sem=send_sem.at[i], recv_sem=recv_sem.at[i],
            device_id=peers[i], device_id_type=pl.DeviceIdType.MESH,
        )

    first = copy(part, r1, 0)
    first.start()
    first.wait()
    mid[...] = part[...] + r1[...]
    second = copy(mid, r2, 1)
    second.start()
    second.wait()
    out[...] = mid[...] + r2[...]


def width_sum(part):
    buffer = pltpu.VMEM(part.shape, part.dtype)
    return pl.pallas_call(
        width_sum_kernel,
        out_shape=jax.ShapeDtypeStruct(part.shape, part.dtype),
        in_specs=[pl.BlockSpec(memory_space=pltpu.VMEM)],
        out_specs=pl.BlockSpec(memory_space=pltpu.VMEM),
        scratch_shapes=[buffer] * 3 + [pltpu.SemaphoreType.DMA((2,))] * 2,
        compiler_params=pltpu.CompilerParams(collective_id=1, has_side_effects=True),
        name="width_sum",
    )(part)


def on_device_pairs(
    cotangent,
    resid_in,
    gate_pre,
    up_pre,
    w_gate,
    w_up,
    w_down,
    norm_gain,
    decoder,
    latent_ids,
    latent_vals,
    attention_mask,
):
    lat_dev = decoder.shape[1]
    local_ix = latent_ids[0] - lax.axis_index("feat") * lat_dev
    inside = (local_ix >= 0) & (local_ix < lat_dev)
    live = attention_mask.astype(jnp.float32)
    weights = jnp.where(inside, latent_vals[0] * live[:, None], 0.0)
    slot_ix = jnp.clip(local_ix, 0, lat_dev - 1)
    coarse = weights.astype(jnp.bfloat16).astype(jnp.float32)
    parts = jnp.concatenate([coarse, weights - coarse], axis=1)
    both = jnp.concatenate([slot_ix, slot_ix], axis=1)
    his = lat_dev // LO
    acts = build_acts(his, both, parts)
    acts, cotangent = lax.optimization_barrier((acts, cotangent))
    grads = chain(
        cotangent, resid_in[0], gate_pre[0], up_pre[0], w_gate[0], w_up[0], w_down[0], norm_gain
    )
    acts, grads = lax.optimization_barrier((acts, grads))
    acts = build_acts(his, both, parts, acts)
    return width_sum(score(grads, decoder[0], acts)).reshape(1, lat_dev)


def solution(mesh):
    in_pairs = mesh.shape["tensor"] == 4 and mesh.shape["feat"] == 2
    body = on_device_pairs if in_pairs else on_device
    return jax.shard_map(
        body,
        mesh=mesh,
        in_specs=(
            P("feat", "tensor"),
            P("pipe", "feat", "tensor"),
            P("pipe", None, "feat"),
            P("pipe", None, "feat"),
            P("pipe", "tensor", "feat"),
            P("pipe", "tensor", "feat"),
            P("pipe", "feat", "tensor"),
            P("pipe", "tensor"),
            P("pipe", "feat", "tensor"),
            P("pipe", None, None),
            P("pipe", None, None),
            P(),
        ),
        out_specs=P("pipe", "feat"),
        check_vma=False,
    )
```
